128 devices in a mesh: row: 16 (over z, x), col: 8 (over y, core).
Axes of the slice: x: 4, y: 4, z: 4, core: 2. Of those that a mesh axis runs over, the one named last changes fastest.
Arguments:
- observed: float32 [8192, 8192], P('row', 'col'), may hold values from -6 to 6
- kernel_rows: float32 [31], replicated, may hold values from 0.01 to 0.1
- kernel_cols: float32 [31], replicated, may hold values from 0.01 to 0.1
- air_temp: float32 [8192, 8192], P('row', 'col'), may hold values from -1 to 1
- wind_speed: float32 [8192, 8192], P('row', 'col'), may hold values from 2 to 8
- net_radiation: float32 [8192, 8192], P('row', 'col'), may hold values from 1.5 to 7
- sentinel: bfloat16 [2, 8192, 8192], P(None, 'row', 'col'), may hold values from 0.049804688 to 1
- block_target: int32 [64, 64], P('row', 'col'), may hold values from 0 to 511, as said below
- land_mask: int32 [8192, 8192], P('row', 'col'), may hold values 0 or 1
Outputs:
- sharpened: float32 [8192, 8192], P('row', 'col')
- sensible: float32 [8192, 8192], P('row', 'col')
- latent: float32 [8192, 8192], P('row', 'col')
The draws below stay inside these ranges and needn't reach their ends.
Inputs may be any that keep to these rules, and one draw needn't show every extreme that they name: Within each column of devices block_target is a bijection onto the blocks of that column; each device sends exactly 2 blocks to each of 16 devices of its column, and none to the others.
All inputs are finite; a program needn't handle non-finite values. No bound on the sum of `land_mask` on one device may be relied on, other than what follows from the above.
Results may differ from the reference program's by a relative error of at most 0.0039.
Values may be sent and summed in bfloat16 or wider, within the bound.
A program may use at most 192 MiB of HBM per device.

```python
import math
import jax
import jax.numpy as jnp
from jax import lax

TILE_ROWS = 512
TILE_COLS = 1024
BLOCK = 128
TAPS = 31
SWEEPS = 3
ROUNDS = 10
CAPACITY = 2
BLOCKS_DEV = 32
PEERS = 16
ROWS = 8192
COLS = 8192
N_ROW = 16
N_COL = 8


def shuffled(key, count, length):
    keys = jax.random.split(key, count)
    return jax.vmap(lambda each: jax.random.permutation(each, length))(keys)


def draw_block_target(key, part):
    key = jax.random.fold_in(key, 7)
    first, second, third = jax.random.split(key, 3)
    per_r = TILE_ROWS // BLOCK
    per_c = TILE_COLS // BLOCK
    offsets = shuffled(first, N_COL, N_ROW)[:, :PEERS]
    source_order = shuffled(second, N_COL * N_ROW, BLOCKS_DEV).reshape(N_COL, N_ROW, BLOCKS_DEV)
    dest_order = shuffled(third, N_COL * N_ROW, BLOCKS_DEV).reshape(N_COL, N_ROW, BLOCKS_DEV)
    which = source_order // CAPACITY
    within = source_order % CAPACITY
    spread = jnp.broadcast_to(offsets[:, None, :], (N_COL, N_ROW, PEERS))
    shift_by = jnp.take_along_axis(spread, which, axis=2)
    rows_idx = jnp.arange(N_ROW, dtype=jnp.int32)[None, :, None]
    cols_idx = jnp.arange(N_COL, dtype=jnp.int32)[:, None, None]
    device = (rows_idx + shift_by) % N_ROW
    slot = dest_order[cols_idx, device, which * CAPACITY + within]
    target = device * BLOCKS_DEV + slot
    target = target.reshape(N_COL, N_ROW, per_r, per_c).transpose(1, 2, 0, 3)
    return target.reshape(N_ROW * per_r, N_COL * per_c).astype(jnp.int32)


def set_ends(values, stream_key, smallest, largest):
    extent = values.shape
    index_at = [jax.random.randint(jax.random.fold_in(stream_key, axis), (), 0, extent[axis]) for axis in range(len(extent))]
    values = values.at[tuple(index_at)].set(smallest)
    longest = extent.index(max(extent))
    index_at[longest] = (index_at[longest] + 1) % extent[longest]
    return values.at[tuple(index_at)].set(largest)


def block_levels(key, shape, cuts, least, high):
    gain = 1.0
    for dim, parts in cuts:
        heights = jax.random.uniform(jax.random.fold_in(jax.random.fold_in(key, 6), dim), (parts,), jnp.float32, least / len(cuts), high / len(cuts))
        gain = gain * jnp.repeat(jnp.exp(heights), shape[dim] // parts).reshape((-1,) + (1,) * (len(shape) - 1 - dim))
    return gain


def bell_draw(key, dims, scale, reach, cuts=(), held_as=jnp.bfloat16):
    drawn = scale * jax.random.normal(key, dims, jnp.float32)
    if cuts:
        drawn = drawn * block_levels(key, dims, cuts, -0.22, 0.18)
    return jnp.clip(drawn, -reach, reach).astype(held_as)


def setup_inputs(seed: int = 0) -> dict:
    splits = jax.random.split(jax.random.key(seed), 10)
    observed = bell_draw(splits[0], (ROWS, COLS), 1.0, 6.0, ((0, 16), (1, 8)), jnp.float32)
    kernel_rows = jnp.clip(jnp.exp(jax.random.uniform(splits[1], (TAPS,), jnp.float32, math.log(0.01), math.log(0.1))), 0.01, 0.1)
    kernel_cols = jnp.clip(jnp.exp(jax.random.uniform(splits[2], (TAPS,), jnp.float32, math.log(0.01), math.log(0.1))), 0.01, 0.1)
    air_temp = jnp.clip(jax.random.uniform(splits[3], (ROWS, COLS), jnp.float32, -1.0, 1.0) * block_levels(splits[3], (ROWS, COLS), ((0, 16), (1, 8)), -0.4, 0.0), -1.0, 1.0)
    wind_speed = jnp.clip(2.0 + 6.0 * jax.random.uniform(splits[4], (ROWS, COLS), jnp.float32) ** block_levels(splits[4], (ROWS, COLS), ((0, 16), (1, 8)), -0.2, 0.2), 2.0, 8.0)
    net_radiation = jnp.clip(1.5 + 5.5 * jax.random.uniform(splits[5], (ROWS, COLS), jnp.float32) ** block_levels(splits[5], (ROWS, COLS), ((0, 16), (1, 8)), -0.2, 0.2), 1.5, 7.0)
    sentinel = jnp.clip(0.049804688 + 0.9501953 * jax.random.uniform(splits[6], (2, ROWS, COLS), jnp.float32) ** block_levels(splits[6], (2, ROWS, COLS), ((1, 16), (2, 8)), -0.2, 0.2), 0.049804688, 1.0).astype(jnp.bfloat16)
    block_target = draw_block_target(jax.random.fold_in(splits[9], 71), 0)
    land_mask = set_ends((jax.random.randint(splits[8], (ROWS, COLS), 0, 4) < 3).astype(jnp.int32), jax.random.fold_in(splits[8], 1), 0, 1)
    return {"observed": observed, "kernel_rows": kernel_rows, "kernel_cols": kernel_cols, "air_temp": air_temp, "wind_speed": wind_speed, "net_radiation": net_radiation, "sentinel": sentinel, "block_target": block_target, "land_mask": land_mask}


RHO_CP = 1206.0
STEP_GAIN = 1.5


def blur_rows(field, kern):
    half = (TAPS - 1) // 2
    padded = jnp.pad(field, ((half, half), (0, 0)))
    count = field.shape[0]
    total = jnp.zeros_like(field)
    for tap in range(TAPS):
        total = total + kern[tap] * padded[tap:tap + count, :]
    return total


def blur_cols(field, kern):
    half = (TAPS - 1) // 2
    padded = jnp.pad(field, ((0, 0), (half, half)))
    count = field.shape[1]
    total = jnp.zeros_like(field)
    for tap in range(TAPS):
        total = total + kern[tap] * padded[:, tap:tap + count]
    return total


def blur(field, row_kernel, col_kernel):
    return blur_cols(blur_rows(field, row_kernel), col_kernel)


def place(sentinel, block_target):
    brow = ROWS // BLOCK
    bcol = COLS // BLOCK
    per_r = TILE_ROWS // BLOCK
    per_c = TILE_COLS // BLOCK
    blocks = sentinel.reshape(2, brow, BLOCK, bcol, BLOCK).transpose(0, 1, 3, 2, 4)
    local = block_target % BLOCKS_DEV
    device = block_target // BLOCKS_DEV
    dest_row = (device * per_r + local // per_c).astype(jnp.int32)
    strip = (jnp.arange(bcol, dtype=jnp.int32) // per_c)[None, :]
    dest_col = (strip * per_c + local % per_c).astype(jnp.int32)
    moved = jnp.zeros_like(blocks).at[:, dest_row, dest_col].set(blocks)
    return moved.transpose(0, 1, 3, 2, 4).reshape(2, ROWS, COLS)


def energy_balance(theta, air, wind, radiation, leaf_raw, cover, land):
    t_rad = 300.0 + 10.0 * theta
    t_air = 300.0 + 10.0 * air
    leaf = 4.0 * leaf_raw
    f_view = 1.0 - jnp.exp(-0.5 * leaf)
    height = 0.1 + 2.0 * cover
    rough = 0.123 * height
    above = 10.0 - 0.67 * height
    log_m = jnp.log(above / rough)
    log_h = jnp.log(7.0 * above / rough)
    net = 100.0 * radiation
    soil_net = net * jnp.exp(-0.45 * leaf)
    ground = 0.35 * soil_net
    celsius = t_air - 273.15
    vapour = 0.6108 * jnp.exp(17.27 * celsius / (celsius + 237.3))
    slope = 4098.0 * vapour / (celsius + 237.3) ** 2
    canopy_h = (net - soil_net) * (1.0 - 1.26 * cover * slope / (slope + 0.066))
    shelter = jnp.exp(-0.5 * leaf)

    def one_round(step, carry):
        zeta, unused_total = carry
        unstable = jnp.minimum(zeta, 0.0)
        stable = jnp.maximum(zeta, 0.0)
        root = (1.0 - 16.0 * unstable) ** 0.25
        psi_m = (2.0 * jnp.log((1.0 + root) / 2.0) + jnp.log((1.0 + root * root) / 2.0)
                 - 2.0 * jnp.arctan(root) + jnp.pi / 2.0 - 5.0 * stable)
        psi_h = 2.0 * jnp.log((1.0 + root * root) / 2.0) - 5.0 * stable
        momentum = log_m - psi_m
        friction = 0.41 * wind / momentum
        resist = momentum * (log_h - psi_h) / (0.41 * 0.41 * wind)
        t_canopy = t_air + canopy_h * resist / RHO_CP
        t_soil = (t_rad - f_view * t_canopy) / (1.0 - f_view)
        soil_res = 1.0 / (0.004 + 0.0288 * friction * shelter)
        soil_h = RHO_CP * (t_soil - t_air) / (resist + soil_res)
        total = canopy_h + soil_h
        target = jnp.clip(-0.41 * 9.81 * above * total / (friction ** 3 * RHO_CP * t_air), -2.0, 0.5)
        return 0.5 * zeta + 0.5 * target, total

    start = (jnp.zeros_like(theta), jnp.zeros_like(theta))
    zeta, total = lax.fori_loop(0, ROUNDS, one_round, start)
    sensible = jnp.where(land == 1, total / 100.0, 0.0)
    latent = jnp.where(land == 1, (net - ground - total) / 100.0, 0.0)
    return sensible, latent


def reference(observed, kernel_rows, kernel_cols, air_temp, wind_speed, net_radiation, sentinel, block_target, land_mask):
    row_kernel = kernel_rows / jnp.sum(kernel_rows)
    col_kernel = kernel_cols / jnp.sum(kernel_cols)
    estimate = observed
    for sweep in range(SWEEPS):
        misfit = observed - blur(estimate, row_kernel, col_kernel)
        estimate = estimate + STEP_GAIN * blur(misfit, row_kernel[::-1], col_kernel[::-1])
    routed = place(sentinel, block_target)
    sensible, latent = energy_balance(estimate, air_temp, wind_speed, net_radiation,
                                      routed[0].astype(jnp.float32), routed[1].astype(jnp.float32), land_mask)
    return estimate, sensible, latent
```

```python
import functools
import math

import jax
import jax.numpy as jnp
from jax import lax
from jax.experimental import pallas as pl
from jax.experimental.pallas import tpu as pltpu
from jax.sharding import PartitionSpec as P

BLOCK = 128
RHO_CP = 1206.0
KARMAN = 0.41
ROUNDS = 10
HALF = 5.0 / 32.0
PSI_M = (0.3186391636950537, 0.2200187838733655, 0.02620018653896533, -0.0003221872048960583,
    -0.00019792193220718868, 1.335036373641197e-05, 2.0235608468337185e-06)
BASE = math.log(7.0) / 2.0 + math.log(2.0 * math.sqrt(HALF))
FIXED = 12


def rcp(v):
    return pl.reciprocal(v, approx=True)


def prepare(theta, air, wind, radiation, leaf_raw, cover):
    t_rad = 300.0 + 10.0 * theta
    t_air = 300.0 + 10.0 * air
    leaf = 4.0 * leaf_raw
    e = jnp.exp(-0.5 * leaf)
    f_view = 1.0 - e
    bare = 1.0 - f_view
    height = 0.1 + 2.0 * cover
    rough = 0.123 * height
    above = 10.0 - 0.67 * height
    log_m = 0.5 * jnp.log(above / rough)
    log_h = 0.5 * jnp.log(7.0 * above / rough)
    net = 100.0 * radiation
    soil_net = net * jnp.exp(-0.45 * leaf)
    ground = 0.35 * soil_net
    celsius = t_air - 273.15
    vapour = 0.6108 * jnp.exp(17.27 * celsius / (celsius + 237.3))
    slope = 4098.0 * vapour / ((celsius + 237.3) * (celsius + 237.3))
    canopy = (net - soil_net) * (1.0 - 1.26 * cover * slope / (slope + 0.066))
    k2w = KARMAN * KARMAN * wind
    beta = (3.6 * KARMAN) * wind * e
    iota = k2w * (1.0 / (0.004 * 4.0))
    c3k = (16.0 * HALF * 9.81 * 4.0 / (RHO_CP * KARMAN * KARMAN)) * above * rcp(wind * wind * wind * t_air)
    held = (log_m + BASE, beta, iota, canopy, c3k, 0.25 * k2w, t_air, t_rad, f_view, bare, net - ground)
    return held, log_m, log_h


def flux(m, h, beta, iota, canopy, c3k, quarter, t_air, t_rad, f_view, bare):
    t_canopy = t_air + canopy * ((m * h) / quarter) / RHO_CP
    t_soil = (t_rad - f_view * t_canopy) / bare
    shifted = m + beta
    return canopy * m + (RHO_CP * (t_soil - t_air)) * (quarter * shifted) * rcp(h * shifted + iota)


def advance(zeta, m, h, *held):
    return 0.5 * zeta + jnp.clip((held[3] * (m * m)) * flux(m, h, *held), -4.0 * HALF, 16.0 * HALF)


def stability(zeta, lm):
    base = lm - jnp.minimum(zeta, 0.0)
    a = jnp.maximum(zeta, 0.0) + HALF
    w = jnp.log(a)
    poly = PSI_M[-1]
    for c in PSI_M[-2:0:-1]:
        poly = poly * w + c
    poly = poly * w + (PSI_M[0] + BASE)
    return base - poly, base - jnp.log(a * lax.rsqrt(a) + math.sqrt(HALF))


def energy_kernel(cfg, place, arrived, theta, air, wind, rad, land, out, sens, lat, held):
    rows, sub, width, unroll, pre = cfg
    step = pl.program_id(0)
    band = theta.shape[0]
    per = BLOCK // band
    cols = theta.shape[1] // BLOCK
    out[...] = theta[...]

    def where(j, r, n):
        return pl.ds(pl.multiple_of(r, n), n), pl.ds(pl.multiple_of(j * BLOCK, BLOCK), BLOCK)

    def fill(t, carry):
        j = t // (band // pre)
        r = (t % (band // pre)) * pre
        slot = place[0, (step // per) * cols + j]
        at = where(j, r, pre)
        inner = pl.multiple_of((slot % 2) * (2 * BLOCK) + (step % per) * band + r, pre)
        leaf = arrived[slot // 2, pl.ds(inner, pre), :].astype(jnp.float32)
        cover = arrived[slot // 2, pl.ds(inner + BLOCK, pre), :].astype(jnp.float32)
        values, m, h = prepare(theta[at], air[at], wind[at], rad[at], leaf, cover)
        for n, v in enumerate(values):
            held[(n, *at)] = v
        held[(11, *at)] = jnp.clip((values[4] * (m * m)) * flux(m, h, *values[1:10]), -4.0 * HALF, 16.0 * HALF)
        return carry

    lax.fori_loop(0, cols * (band // pre), fill, 0)

    def col(t, carry):
        pieces = []
        for q in range(width):
            tt = t * width + q
            j = tt // (band // rows)
            r = (tt % (band // rows)) * rows
            for s in range(rows // sub):
                pieces.append(where(j, r + s * sub, sub))

        def one(i, zetas):
            new = []
            for at, zeta in zip(pieces, zetas):
                m, h = stability(zeta, held[(0, *at)])
                new.append(advance(zeta, m, h, *(held[(n, *at)] for n in range(1, 10))))
            return tuple(new)

        zetas = lax.fori_loop(0, ROUNDS - 2, one, tuple(held[(11, *at)] for at in pieces), unroll=unroll)
        for at, zeta in zip(pieces, zetas):
            m, h = stability(zeta, held[(0, *at)])
            total = flux(m, h, *(held[(n, *at)] for n in range(1, 10))) / m
            keep = land[at] == 1
            sens[at] = jnp.where(keep, 0.01 * total, 0.0)
            lat[at] = jnp.where(keep, 0.01 * (held[(10, *at)] - total), 0.0)
        return carry

    lax.fori_loop(0, cols * (band // rows) // width, col, 0)


def energy(place, arrived, theta, air, wind, rad, land, band=128, rows=128, sub=16, width=1, unroll=4, pre=64):
    shape = theta.shape
    spec = pl.BlockSpec((band, shape[1]), lambda i, place: (i, 0))
    return pl.pallas_call(
        functools.partial(energy_kernel, (rows, sub, width, unroll, pre)),
        grid_spec=pltpu.PrefetchScalarGridSpec(
            num_scalar_prefetch=1,
            grid=(shape[0] // band,),
            in_specs=[pl.BlockSpec(arrived.shape, lambda i, place: (0, 0, 0))] + [spec] * 5,
            out_specs=[spec] * 3,
            scratch_shapes=[pltpu.VMEM((FIXED, band, shape[1]), jnp.float32)],
        ),
        out_shape=[jax.ShapeDtypeStruct(shape, jnp.float32)] * 3,
        compiler_params=pltpu.CompilerParams(vmem_limit_bytes=48 << 20),
        name="energy",
    )(place, arrived, theta, air, wind, rad, land)


TAPS = 31
SPAN = TAPS // 2
STEP_GAIN = 1.5
MESH = pl.DeviceIdType.MESH
FRAME = 96
EDGE = 128
TAIL = 16
WINDOW = 256
TALL = 192


def split(value):
    first = value.astype(jnp.bfloat16)
    rest = value - first.astype(jnp.float32)
    second = rest.astype(jnp.bfloat16)
    return first, second, (rest - second.astype(jnp.float32)).astype(jnp.bfloat16)


def mul(a, b):
    return jnp.dot(a, b, preferred_element_type=jnp.float32)


def precise(a, b):
    a1, a2, a3 = split(a)
    b1, b2, b3 = split(b)
    return mul(a1, b1) + ((mul(a2, b1) + mul(a1, b2)) + (mul(a2, b2) + (mul(a3, b1) + mul(a1, b3))))


def taps_matrix(out, taps, rows, cols, offset, sign):
    total = taps[0]
    for t in range(1, TAPS):
        total = total + taps[t]
    part = 64

    def fill(n, carry):
        at = pl.multiple_of(n * part, part)
        i = lax.broadcasted_iota(jnp.int32, (part, cols), 0) + at
        j = lax.broadcasted_iota(jnp.int32, (part, cols), 1)
        which = offset + sign * (i - j)
        acc = jnp.zeros((part, cols), jnp.float32)
        for t in range(TAPS):
            acc = jnp.where(which == t, taps[t], acc)
        out[pl.ds(at, part), :cols] = acc / jnp.full((part, cols), total, jnp.float32)
        return carry

    lax.fori_loop(0, rows // part, fill, 0)


def inside(shape, dim, first, size):
    at = lax.broadcasted_iota(jnp.int32, shape, dim) + first
    return (at >= 0) & (at < size)


def sweep_kernel(
    n_row, n_col, krow_any, kcol_any, target_any, observed, sentinel, sharp, arrived, place,
    krow, kcol, target, pool, outbox, wide, flat, mid, midb, state, nudge, first, second,
    row_g, row_b, col_g, col_b, labels, halo_send, halo_recv, block_send, block_recv, local_sem,
):
    row, col = lax.axis_index("row"), lax.axis_index("col")
    tile_rows, tile_cols = observed.shape
    per_c = tile_cols // BLOCK
    blocks = (tile_rows // BLOCK) * per_c
    rows, cols = tile_rows + 2 * FRAME, tile_cols + 2 * EDGE
    row0, col0 = row * tile_rows, col * tile_cols
    scene_rows, scene_cols = n_row * tile_rows, n_col * tile_cols
    sides = [(dr, dc) for dr in (-1, 0, 1) for dc in (-1, 0, 1) if (dr, dc) != (0, 0)]

    def shifted(dr, dc):
        return lax.rem(row + (dr + n_row), n_row), lax.rem(col + (dc + n_col), n_col)

    barrier = pltpu.get_barrier_semaphore()
    for dr, dc in sides:
        if dc != 0:
            pl.semaphore_signal(barrier, inc=1, device_id=shifted(dr, dc), device_id_type=MESH)

    def greet(k, carry):
        pl.semaphore_signal(barrier, inc=1, device_id=(lax.rem(row + k, n_row), col), device_id_type=MESH)
        return carry

    lax.fori_loop(1, n_row, greet, 0)
    for n, (source, held) in enumerate(((target_any, target), (krow_any, krow), (kcol_any, kcol))):
        pltpu.make_async_copy(source, held, local_sem.at[3 + n]).start()

    def gather(n, carry):
        at = (pl.ds(pl.multiple_of((n // per_c) * BLOCK, BLOCK), BLOCK), pl.ds(pl.multiple_of((n % per_c) * BLOCK, BLOCK), BLOCK))
        for ch in range(2):
            pltpu.make_async_copy(sentinel.at[(ch, *at)], pool.at[n, pl.ds(ch * BLOCK, BLOCK), :], local_sem.at[6]).start()
        return carry

    lax.fori_loop(0, blocks, gather, 0)
    own = pltpu.make_async_copy(observed, wide.at[pl.ds(FRAME, tile_rows), pl.ds(EDGE, tile_cols)], local_sem.at[0])
    own.start()
    pl.semaphore_wait(barrier, 6 + n_row - 1)

    def span(d, length, frame):
        if d == 0:
            return pl.ds(0, length), pl.ds(frame, length)
        if d > 0:
            return pl.ds(length - frame, frame), pl.ds(0, frame)
        return pl.ds(0, frame), pl.ds(frame + length, frame)

    halos = []
    for n, (dr, dc) in enumerate(sides):
        src_r, dst_r = span(dr, tile_rows, FRAME)
        src_c, dst_c = span(dc, tile_cols, EDGE)
        halos.append(pltpu.make_async_remote_copy(
            src_ref=observed.at[src_r, src_c],
            dst_ref=wide.at[dst_r, dst_c],
            send_sem=halo_send.at[n],
            recv_sem=halo_recv.at[n],
            device_id=shifted(dr, dc),
            device_id_type=MESH,
        ))
    for halo in halos:
        halo.start()

    pltpu.make_async_copy(target_any, target, local_sem.at[3]).wait()
    pltpu.make_async_copy(pool, pool, local_sem.at[6]).wait()

    def pack(k):
        dest = lax.rem(row + k, n_row)

        def scan(n, found):
            low, high, low_tag, high_tag = found
            aim = target[n // per_c, n % per_c]
            here = aim // blocks == dest
            earlier = here & (low > n)
            return (
                jnp.where(earlier, n, low), jnp.where(here, n, high),
                jnp.where(earlier, aim, low_tag), jnp.where(here, aim, high_tag),
            )

        start = (jnp.int32(blocks - 1), jnp.int32(0), jnp.int32(0), jnp.int32(0))
        low, high, low_tag, high_tag = lax.fori_loop(0, blocks, scan, start, unroll=8)
        line = lax.broadcasted_iota(jnp.int32, (TAIL, BLOCK), 0)
        tags = jnp.zeros((TAIL, BLOCK), jnp.float32)
        for which, (n, tag) in enumerate(((low, low_tag), (high, high_tag))):
            outbox[k, pl.ds(2 * which * BLOCK, 2 * BLOCK), :] = pool[n]
            tags = jnp.where(line == which, lax.rem(tag, blocks).astype(jnp.float32), tags)
        outbox[k, pl.ds(4 * BLOCK, TAIL), :] = tags.astype(jnp.bfloat16)

    def parcel(k):
        return pltpu.make_async_remote_copy(
            src_ref=outbox.at[k],
            dst_ref=arrived.at[row],
            send_sem=block_send.at[k],
            recv_sem=block_recv.at[k],
            device_id=(lax.rem(row + k, n_row), col),
            device_id_type=MESH,
        )

    def post(k, carry):
        pack(k)
        parcel(k).start()
        return carry

    lax.fori_loop(1, n_row, post, 0)
    pack(0)
    kept = pltpu.make_async_copy(outbox.at[0], arrived.at[row], local_sem.at[1])
    kept.start()

    for n, (source, held) in enumerate(((krow_any, krow), (kcol_any, kcol))):
        pltpu.make_async_copy(source, held, local_sem.at[4 + n]).wait()
    half = WINDOW // 4
    taps_matrix(first, krow, TALL, WINDOW, 47, 1)
    taps_matrix(second, krow, WINDOW, WINDOW, SPAN, -1)
    row_b[:TALL, :], row_b[TALL:2 * TALL, :], row_b[2 * TALL:, :] = split(first[:TALL, :])
    starts = (-64, -32, 0, 416, 352, 384)
    for n, start in enumerate((None, *starts)):
        left = first[:TALL, :]
        if start is not None:
            left = jnp.where(inside((TALL, WINDOW), 1, row0 + (start - FRAME // 3), scene_rows), left, 0.0)
        row_g[n, :TALL, :], row_g[n, TALL:2 * TALL, :], row_g[n, 2 * TALL:, :] = split(precise(left, second[...]))
    taps_matrix(first, kcol, WINDOW, BLOCK, half + SPAN, -1)
    taps_matrix(second, kcol, WINDOW, WINDOW, SPAN, 1)
    col_b[:, :BLOCK], col_b[:, BLOCK:2 * BLOCK], col_b[:, 2 * BLOCK:] = split(first[:, :BLOCK])
    for n, start in enumerate((None, 0, tile_cols - BLOCK)):
        right = first[:, :BLOCK]
        if start is not None:
            right = jnp.where(inside((WINDOW, BLOCK), 0, col0 + (start - half), scene_cols), right, 0.0)
        col_g[n, :, :BLOCK], col_g[n, :, BLOCK:2 * BLOCK], col_g[n, :, 2 * BLOCK:] = split(precise(second[...], right))
    for ref in (mid, midb):
        for n in range(3):
            ref[n, pl.ds(rows, 32), :] = jnp.zeros((32, cols), jnp.bfloat16)

    own.wait()
    for halo in halos:
        halo.wait()

    def flatten(source, height, masked):
        part = 64

        def piece(n, carry):
            at = pl.ds(pl.multiple_of(n * part, part), part)
            lane = lax.broadcasted_iota(jnp.int32, (part, BLOCK), 1)
            before = jnp.zeros((part, BLOCK), jnp.float32)
            for t in range(cols // BLOCK + 1):
                if t < cols // BLOCK:
                    value = source[at, pl.ds(t * BLOCK, BLOCK)]
                    if masked:
                        value = jnp.where(
                            inside((part, BLOCK), 0, row0 + (n * part - FRAME), scene_rows)
                            & inside((part, BLOCK), 1, col0 + (t * BLOCK - EDGE), scene_cols), value, 0.0)
                        source[at, pl.ds(t * BLOCK, BLOCK)] = value
                    turned = pltpu.roll(value, BLOCK // 2, 1)
                else:
                    turned = jnp.zeros((part, BLOCK), jnp.float32)
                for q, part_q in enumerate(split(jnp.where(lane < BLOCK // 2, before, turned))):
                    flat[q, at, pl.ds(t * BLOCK, BLOCK)] = part_q
                before = turned
            return carry

        lax.fori_loop(0, height // part, piece, 0)

    def along_cols(height, begin, end, both):
        def block(j, carry):
            at = pl.ds(pl.multiple_of(j * BLOCK, BLOCK), WINDOW)
            put = (pl.ds(0, height), pl.ds(pl.multiple_of(j * BLOCK, BLOCK), BLOCK))
            kind = jnp.where(j == 1, 1, jnp.where(j == per_c, 2, 0))
            x1, x2, x3 = (flat[q, pl.ds(0, height), at] for q in range(3))

            def apply(weights, to):
                got = mul(x2, weights[:, :2 * BLOCK]) + mul(x1, weights[:, :2 * BLOCK])
                small = mul(x3, weights[:, :BLOCK]) + mul(x1, weights[:, 2 * BLOCK:])
                for q, part_q in enumerate(split(got[:, :BLOCK] + (got[:, BLOCK:] + small))):
                    to[(q, *put)] = part_q

            apply(col_g[kind], mid)
            if both:
                apply(col_b[...], midb)
            return carry

        lax.fori_loop(begin, end, block, 0)

    def along_rows(weights, source, at, length):
        top = mul(weights, source[(0, *at)])
        more = mul(weights[:2 * TALL, :], source[(1, *at)])
        least = mul(weights[:TALL, :], source[(2, *at)])
        small = (top[2 * TALL:2 * TALL + length] + more[TALL:TALL + length]) + least[:length]
        return top[:length] + ((top[TALL:TALL + length] + more[:length]) + small)

    def update(start, sizes, kinds, before, shift, height, after, begin, end):
        offset = 0
        for size, kind in zip(sizes, kinds):
            def strip(n, carry, offset=offset, size=size, kind=kind):
                across = pl.ds(pl.multiple_of(n * WINDOW, WINDOW) + begin, WINDOW)
                at = (pl.ds(offset, WINDOW), across)
                blurred = along_rows(row_g[kind], mid, at, size)
                if start == -64:
                    extra = along_rows(row_b[...], midb, at, size)
                    nudge[pl.ds(offset, size), across] = extra
                else:
                    extra = nudge[pl.ds(offset + start + 64, size), across]
                value = before[pl.ds(offset + shift, size), across] + STEP_GAIN * (extra - blurred)
                if start == 0:
                    after[pl.ds(offset, size), pl.ds(pl.multiple_of(n * WINDOW, WINDOW), WINDOW)] = value
                else:
                    after[pl.ds(offset, size), across] = jnp.where(
                        inside((size, WINDOW), 0, row0 + (start + offset), scene_rows)
                        & inside((size, WINDOW), 1, col0 + (n * WINDOW - EDGE), scene_cols), value, 0.0)
                return carry

            lax.fori_loop(0, (end - begin) // WINDOW, strip, 0)
            offset += size

    flatten(wide, rows, True)
    along_cols(rows, 0, cols // BLOCK, True)
    update(-64, (160, 160, 160, 160), (1, 0, 0, 4), wide, 32, rows - 64, state, 0, cols)
    flatten(state, rows - 64, False)
    along_cols(rows - 64, 0, cols // BLOCK, False)
    update(-32, (192, 192, 192), (2, 0, 5), state, 32, rows - 128, wide, 0, cols)
    flatten(wide, rows - 128, False)
    along_cols(rows - 128, 1, 1 + per_c, False)
    update(0, (192, 192, 128), (3, 0, 6), wide, 32, tile_rows, sharp, EDGE, EDGE + tile_cols)

    kept.wait()

    def collect(k, carry):
        parcel(k).wait()
        return carry

    lax.fori_loop(1, n_row, collect, 0)
    fetch = pltpu.make_async_copy(arrived.at[:, pl.ds(4 * BLOCK, TAIL), :], labels, local_sem.at[2])
    fetch.start()
    fetch.wait()
    lane = lax.broadcasted_iota(jnp.int32, (1, BLOCK), 1)
    found = jnp.zeros((1, BLOCK), jnp.int32)
    for r in range(n_row):
        for which in range(2):
            tag = labels[r][which:which + 1, :].astype(jnp.float32).astype(jnp.int32)
            found = jnp.where(tag == lane, 2 * r + which, found)
    place[...] = found


def sweeps(n_row, n_col, krow, kcol, target, observed, sentinel):
    tile_rows, tile_cols = observed.shape
    rows, cols = tile_rows + 2 * FRAME, tile_cols + 2 * EDGE
    f32, b16 = jnp.float32, jnp.bfloat16
    vmem = pl.BlockSpec(memory_space=pltpu.VMEM)
    any_ = pl.BlockSpec(memory_space=pl.ANY)
    parcel = 4 * BLOCK + TAIL
    return pl.pallas_call(
        functools.partial(sweep_kernel, n_row, n_col),
        in_specs=[any_] * 5,
        out_specs=[vmem, any_, vmem],
        out_shape=[
            jax.ShapeDtypeStruct((tile_rows, tile_cols), f32),
            jax.ShapeDtypeStruct((n_row, parcel, BLOCK), b16),
            jax.ShapeDtypeStruct((1, BLOCK), jnp.int32),
        ],
        scratch_shapes=[
            pltpu.SMEM(krow.shape, f32),
            pltpu.SMEM(kcol.shape, f32),
            pltpu.SMEM(target.shape, jnp.int32),
            pltpu.VMEM((target.size, 2 * BLOCK, BLOCK), b16),
            pltpu.VMEM((n_row, parcel, BLOCK), b16),
            pltpu.VMEM((rows, cols), f32),
            pltpu.VMEM((3, rows, cols + BLOCK), b16),
            pltpu.VMEM((3, rows + 32, cols), b16),
            pltpu.VMEM((3, rows + 32, cols), b16),
            pltpu.VMEM((rows - 64, cols), f32),
            pltpu.VMEM((rows - 64, cols), f32),
            pltpu.VMEM((WINDOW, WINDOW), f32),
            pltpu.VMEM((WINDOW, WINDOW), f32),
            pltpu.VMEM((7, 3 * TALL, WINDOW), b16),
            pltpu.VMEM((3 * TALL, WINDOW), b16),
            pltpu.VMEM((3, WINDOW, 3 * BLOCK), b16),
            pltpu.VMEM((WINDOW, 3 * BLOCK), b16),
            pltpu.VMEM((n_row, TAIL, BLOCK), b16),
            pltpu.SemaphoreType.DMA((8,)),
            pltpu.SemaphoreType.DMA((8,)),
            pltpu.SemaphoreType.DMA((n_row,)),
            pltpu.SemaphoreType.DMA((n_row,)),
            pltpu.SemaphoreType.DMA((7,)),
        ],
        compiler_params=pltpu.CompilerParams(collective_id=0, has_side_effects=True, vmem_limit_bytes=48 << 20),
        name="sweeps",
    )(krow, kcol, target, observed, sentinel)


def local(n_row, n_col, observed, kernel_rows, kernel_cols, air_temp, wind_speed, net_radiation, sentinel, block_target, land_mask):
    theta, arrived, place = sweeps(n_row, n_col, kernel_rows, kernel_cols, block_target, observed, sentinel)
    return energy(place, arrived, theta, air_temp, wind_speed, net_radiation, land_mask)


def solution(mesh):
    tile = P("row", "col")
    return jax.shard_map(
        functools.partial(local, mesh.shape["row"], mesh.shape["col"]),
        mesh=mesh,
        in_specs=(tile, P(), P(), tile, tile, tile, P(None, "row", "col"), tile, tile),
        out_specs=(tile, tile, tile),
        check_vma=False,
    )
```

```python
import functools
import math

import jax
import jax.numpy as jnp
from jax import lax
from jax.experimental import pallas as pl
from jax.experimental.pallas import tpu as pltpu
from jax.sharding import PartitionSpec as P

BLOCK = 128
RHO_CP = 1206.0
KARMAN = 0.41
ROUNDS = 10
HALF = 5.0 / 32.0
PSI_M = (0.3186391636950537, 0.2200187838733655, 0.02620018653896533, -0.0003221872048960583,
    -0.00019792193220718868, 1.335036373641197e-05, 2.0235608468337185e-06)
BASE = math.log(7.0) / 2.0 + math.log(2.0 * math.sqrt(HALF))
FIXED = 12


def rcp(v):
    return pl.reciprocal(v, approx=True)


def prepare(theta, air, wind, radiation, leaf_raw, cover):
    t_rad = 300.0 + 10.0 * theta
    t_air = 300.0 + 10.0 * air
    leaf = 4.0 * leaf_raw
    e = jnp.exp(-0.5 * leaf)
    f_view = 1.0 - e
    bare = 1.0 - f_view
    height = 0.1 + 2.0 * cover
    rough = 0.123 * height
    above = 10.0 - 0.67 * height
    log_m = 0.5 * jnp.log(above / rough)
    log_h = 0.5 * jnp.log(7.0 * above / rough)
    net = 100.0 * radiation
    soil_net = net * jnp.exp(-0.45 * leaf)
    ground = 0.35 * soil_net
    celsius = t_air - 273.15
    vapour = 0.6108 * jnp.exp(17.27 * celsius / (celsius + 237.3))
    slope = 4098.0 * vapour / ((celsius + 237.3) * (celsius + 237.3))
    canopy = (net - soil_net) * (1.0 - 1.26 * cover * slope / (slope + 0.066))
    k2w = KARMAN * KARMAN * wind
    beta = (3.6 * KARMAN) * wind * e
    iota = k2w * (1.0 / (0.004 * 4.0))
    c3k = (16.0 * HALF * 9.81 * 4.0 / (RHO_CP * KARMAN * KARMAN)) * above * rcp(wind * wind * wind * t_air)
    held = (log_m + BASE, beta, iota, canopy, c3k, 0.25 * k2w, t_air, t_rad, f_view, bare, net - ground)
    return held, log_m, log_h


def flux(m, h, beta, iota, canopy, c3k, quarter, t_air, t_rad, f_view, bare):
    t_canopy = t_air + canopy * ((m * h) / quarter) / RHO_CP
    t_soil = (t_rad - f_view * t_canopy) / bare
    shifted = m + beta
    return canopy * m + (RHO_CP * (t_soil - t_air)) * (quarter * shifted) * rcp(h * shifted + iota)


def advance(zeta, m, h, *held):
    return 0.5 * zeta + jnp.clip((held[3] * (m * m)) * flux(m, h, *held), -4.0 * HALF, 16.0 * HALF)


def stability(zeta, lm):
    base = lm - jnp.minimum(zeta, 0.0)
    a = jnp.maximum(zeta, 0.0) + HALF
    w = jnp.log(a)
    poly = PSI_M[-1]
    for c in PSI_M[-2:0:-1]:
        poly = poly * w + c
    poly = poly * w + (PSI_M[0] + BASE)
    return base - poly, base - jnp.log(a * lax.rsqrt(a) + math.sqrt(HALF))


def energy_kernel(cfg, place, arrived, theta, air, wind, rad, land, out, sens, lat, held):
    rows, sub, width, unroll, pre = cfg
    step = pl.program_id(0)
    band = theta.shape[0]
    per = BLOCK // band
    cols = theta.shape[1] // BLOCK
    out[...] = theta[...]

    def where(j, r, n):
        return pl.ds(pl.multiple_of(r, n), n), pl.ds(pl.multiple_of(j * BLOCK, BLOCK), BLOCK)

    def fill(t, carry):
        j = t // (band // pre)
        r = (t % (band // pre)) * pre
        slot = place[0, (step // per) * cols + j]
        at = where(j, r, pre)
        inner = pl.multiple_of((slot % 2) * (2 * BLOCK) + (step % per) * band + r, pre)
        leaf = arrived[slot // 2, pl.ds(inner, pre), :].astype(jnp.float32)
        cover = arrived[slot // 2, pl.ds(inner + BLOCK, pre), :].astype(jnp.float32)
        values, m, h = prepare(theta[at], air[at], wind[at], rad[at], leaf, cover)
        for n, v in enumerate(values):
            held[(n, *at)] = v
        held[(11, *at)] = jnp.clip((values[4] * (m * m)) * flux(m, h, *values[1:10]), -4.0 * HALF, 16.0 * HALF)
        return carry

    lax.fori_loop(0, cols * (band // pre), fill, 0)

    def col(t, carry):
        pieces = []
        for q in range(width):
            tt = t * width + q
            j = tt // (band // rows)
            r = (tt % (band // rows)) * rows
            for s in range(rows // sub):
                pieces.append(where(j, r + s * sub, sub))

        def one(i, zetas):
            new = []
            for at, zeta in zip(pieces, zetas):
                m, h = stability(zeta, held[(0, *at)])
                new.append(advance(zeta, m, h, *(held[(n, *at)] for n in range(1, 10))))
            return tuple(new)

        zetas = lax.fori_loop(0, ROUNDS - 2, one, tuple(held[(11, *at)] for at in pieces), unroll=unroll)
        for at, zeta in zip(pieces, zetas):
            m, h = stability(zeta, held[(0, *at)])
            total = flux(m, h, *(held[(n, *at)] for n in range(1, 10))) / m
            keep = land[at] == 1
            sens[at] = jnp.where(keep, 0.01 * total, 0.0)
            lat[at] = jnp.where(keep, 0.01 * (held[(10, *at)] - total), 0.0)
        return carry

    lax.fori_loop(0, cols * (band // rows) // width, col, 0)


def energy(place, arrived, theta, air, wind, rad, land, band=128, rows=128, sub=16, width=1, unroll=4, pre=64):
    shape = theta.shape
    spec = pl.BlockSpec((band, shape[1]), lambda i, place: (i, 0))
    return pl.pallas_call(
        functools.partial(energy_kernel, (rows, sub, width, unroll, pre)),
        grid_spec=pltpu.PrefetchScalarGridSpec(
            num_scalar_prefetch=1,
            grid=(shape[0] // band,),
            in_specs=[pl.BlockSpec(arrived.shape, lambda i, place: (0, 0, 0))] + [spec] * 5,
            out_specs=[spec] * 3,
            scratch_shapes=[pltpu.VMEM((FIXED, band, shape[1]), jnp.float32)],
        ),
        out_shape=[jax.ShapeDtypeStruct(shape, jnp.float32)] * 3,
        compiler_params=pltpu.CompilerParams(vmem_limit_bytes=48 << 20),
        name="energy",
    )(place, arrived, theta, air, wind, rad, land)


TAPS = 31
SPAN = TAPS // 2
STEP_GAIN = 1.5
MESH = pl.DeviceIdType.MESH
FRAME = 96
EDGE = 128
TAIL = 16
WINDOW = 256
TALL = 192


def split(value):
    first = value.astype(jnp.bfloat16)
    rest = value - first.astype(jnp.float32)
    second = rest.astype(jnp.bfloat16)
    return first, second, (rest - second.astype(jnp.float32)).astype(jnp.bfloat16)


def mul(a, b):
    return jnp.dot(a, b, preferred_element_type=jnp.float32)


def precise(a, b):
    a1, a2, a3 = split(a)
    b1, b2, b3 = split(b)
    return mul(a1, b1) + ((mul(a2, b1) + mul(a1, b2)) + (mul(a2, b2) + (mul(a3, b1) + mul(a1, b3))))


def taps_matrix(out, taps, rows, cols, offset, sign):
    total = taps[0]
    for t in range(1, TAPS):
        total = total + taps[t]
    part = 64

    def fill(n, carry):
        at = pl.multiple_of(n * part, part)
        i = lax.broadcasted_iota(jnp.int32, (part, cols), 0) + at
        j = lax.broadcasted_iota(jnp.int32, (part, cols), 1)
        which = offset + sign * (i - j)
        acc = jnp.zeros((part, cols), jnp.float32)
        for t in range(TAPS):
            acc = jnp.where(which == t, taps[t], acc)
        out[pl.ds(at, part), :cols] = acc / jnp.full((part, cols), total, jnp.float32)
        return carry

    lax.fori_loop(0, rows // part, fill, 0)


def inside(shape, dim, first, size):
    at = lax.broadcasted_iota(jnp.int32, shape, dim) + first
    return (at >= 0) & (at < size)


def sweep_kernel(
    n_row, n_col, krow_any, kcol_any, target_any, observed, sentinel, sharp, arrived, place,
    krow, kcol, target, pool, outbox, wide, flat, mid, midb, state, nudge, first, second,
    row_g, row_b, col_g, col_b, labels, halo_send, halo_recv, block_send, block_recv, local_sem,
):
    row, col = lax.axis_index("row"), lax.axis_index("col")
    tile_rows, tile_cols = observed.shape
    per_c = tile_cols // BLOCK
    blocks = (tile_rows // BLOCK) * per_c
    rows, cols = tile_rows + 2 * FRAME, tile_cols + 2 * EDGE
    row0, col0 = row * tile_rows, col * tile_cols
    scene_rows, scene_cols = n_row * tile_rows, n_col * tile_cols
    sides = [(dr, dc) for dr in (-1, 0, 1) for dc in (-1, 0, 1) if (dr, dc) != (0, 0)]

    def shifted(dr, dc):
        return lax.rem(row + (dr + n_row), n_row), lax.rem(col + (dc + n_col), n_col)

    barrier = pltpu.get_barrier_semaphore()
    for dr, dc in sides:
        if dc != 0:
            pl.semaphore_signal(barrier, inc=1, device_id=shifted(dr, dc), device_id_type=MESH)

    def greet(k, carry):
        pl.semaphore_signal(barrier, inc=1, device_id=(lax.rem(row + k, n_row), col), device_id_type=MESH)
        return carry

    lax.fori_loop(1, n_row, greet, 0)
    for n, (source, held) in enumerate(((target_any, target), (krow_any, krow), (kcol_any, kcol))):
        pltpu.make_async_copy(source, held, local_sem.at[3 + n]).start()

    def gather(n, carry):
        at = (pl.ds(pl.multiple_of((n // per_c) * BLOCK, BLOCK), BLOCK), pl.ds(pl.multiple_of((n % per_c) * BLOCK, BLOCK), BLOCK))
        for ch in range(2):
            pltpu.make_async_copy(sentinel.at[(ch, *at)], pool.at[n, pl.ds(ch * BLOCK, BLOCK), :], local_sem.at[6]).start()
        return carry

    lax.fori_loop(0, blocks, gather, 0)
    own = pltpu.make_async_copy(observed, wide.at[pl.ds(FRAME, tile_rows), pl.ds(EDGE, tile_cols)], local_sem.at[0])
    own.start()
    pl.semaphore_wait(barrier, 6 + n_row - 1)

    def span(d, length, frame):
        if d == 0:
            return pl.ds(0, length), pl.ds(frame, length)
        if d > 0:
            return pl.ds(length - frame, frame), pl.ds(0, frame)
        return pl.ds(0, frame), pl.ds(frame + length, frame)

    halos = []
    for n, (dr, dc) in enumerate(sides):
        src_r, dst_r = span(dr, tile_rows, FRAME)
        src_c, dst_c = span(dc, tile_cols, EDGE)
        halos.append(pltpu.make_async_remote_copy(
            src_ref=observed.at[src_r, src_c],
            dst_ref=wide.at[dst_r, dst_c],
            send_sem=halo_send.at[n],
            recv_sem=halo_recv.at[n],
            device_id=shifted(dr, dc),
            device_id_type=MESH,
        ))
    for halo in halos:
        halo.start()

    pltpu.make_async_copy(target_any, target, local_sem.at[3]).wait()
    pltpu.make_async_copy(pool, pool, local_sem.at[6]).wait()

    def pack(k):
        dest = lax.rem(row + k, n_row)

        def scan(n, found):
            low, high, low_tag, high_tag = found
            aim = target[n // per_c, n % per_c]
            here = aim // blocks == dest
            earlier = here & (low > n)
            return (
                jnp.where(earlier, n, low), jnp.where(here, n, high),
                jnp.where(earlier, aim, low_tag), jnp.where(here, aim, high_tag),
            )

        start = (jnp.int32(blocks - 1), jnp.int32(0), jnp.int32(0), jnp.int32(0))
        low, high, low_tag, high_tag = lax.fori_loop(0, blocks, scan, start, unroll=8)
        line = lax.broadcasted_iota(jnp.int32, (TAIL, BLOCK), 0)
        tags = jnp.zeros((TAIL, BLOCK), jnp.float32)
        for which, (n, tag) in enumerate(((low, low_tag), (high, high_tag))):
            outbox[k, pl.ds(2 * which * BLOCK, 2 * BLOCK), :] = pool[n]
            tags = jnp.where(line == which, lax.rem(tag, blocks).astype(jnp.float32), tags)
        outbox[k, pl.ds(4 * BLOCK, TAIL), :] = tags.astype(jnp.bfloat16)

    def parcel(k):
        return pltpu.make_async_remote_copy(
            src_ref=outbox.at[k],
            dst_ref=arrived.at[row],
            send_sem=block_send.at[k],
            recv_sem=block_recv.at[k],
            device_id=(lax.rem(row + k, n_row), col),
            device_id_type=MESH,
        )

    def post(k, carry):
        pack(k)
        parcel(k).start()
        return carry

    lax.fori_loop(1, n_row, post, 0)
    pack(0)
    kept = pltpu.make_async_copy(outbox.at[0], arrived.at[row], local_sem.at[1])
    kept.start()

    for n, (source, held) in enumerate(((krow_any, krow), (kcol_any, kcol))):
        pltpu.make_async_copy(source, held, local_sem.at[4 + n]).wait()
    half = WINDOW // 4
    taps_matrix(first, krow, TALL, WINDOW, 47, 1)
    taps_matrix(second, krow, WINDOW, WINDOW, SPAN, -1)
    row_b[:TALL, :], row_b[TALL:2 * TALL, :], row_b[2 * TALL:, :] = split(first[:TALL, :])
    starts = (-64, -32, 0, 416, 352, 384)
    for n, start in enumerate((None, *starts)):
        def make_rows(n=n, start=start):
            left = first[:TALL, :]
            if start is not None:
                left = jnp.where(inside((TALL, WINDOW), 1, row0 + (start - FRAME // 3), scene_rows), left, 0.0)
            row_g[n, :TALL, :], row_g[n, TALL:2 * TALL, :], row_g[n, 2 * TALL:, :] = split(precise(left, second[...]))

        if start is None:
            make_rows()
        else:
            pl.when(row == (0 if n < 4 else n_row - 1))(make_rows)
    taps_matrix(first, kcol, WINDOW, BLOCK, half + SPAN, -1)
    taps_matrix(second, kcol, WINDOW, WINDOW, SPAN, 1)
    col_b[:, :BLOCK], col_b[:, BLOCK:2 * BLOCK], col_b[:, 2 * BLOCK:] = split(first[:, :BLOCK])
    for n, start in enumerate((None, 0, tile_cols - BLOCK)):
        def make_cols(n=n, start=start):
            right = first[:, :BLOCK]
            if start is not None:
                right = jnp.where(inside((WINDOW, BLOCK), 0, col0 + (start - half), scene_cols), right, 0.0)
            col_g[n, :, :BLOCK], col_g[n, :, BLOCK:2 * BLOCK], col_g[n, :, 2 * BLOCK:] = split(precise(second[...], right))

        if start is None:
            make_cols()
        else:
            pl.when(col == (0 if n == 1 else n_col - 1))(make_cols)
    for ref in (mid, midb):
        for n in range(3):
            ref[n, pl.ds(rows, 32), :] = jnp.zeros((32, cols), jnp.bfloat16)

    own.wait()
    for halo in halos:
        halo.wait()

    def flatten(source, height, masked):
        part = 64

        def piece(n, carry):
            at = pl.ds(pl.multiple_of(n * part, part), part)
            lane = lax.broadcasted_iota(jnp.int32, (part, BLOCK), 1)
            before = jnp.zeros((part, BLOCK), jnp.float32)
            for t in range(cols // BLOCK + 1):
                if t < cols // BLOCK:
                    value = source[at, pl.ds(t * BLOCK, BLOCK)]
                    if masked:
                        value = jnp.where(
                            inside((part, BLOCK), 0, row0 + (n * part - FRAME), scene_rows)
                            & inside((part, BLOCK), 1, col0 + (t * BLOCK - EDGE), scene_cols), value, 0.0)
                        source[at, pl.ds(t * BLOCK, BLOCK)] = value
                    turned = pltpu.roll(value, BLOCK // 2, 1)
                else:
                    turned = jnp.zeros((part, BLOCK), jnp.float32)
                for q, part_q in enumerate(split(jnp.where(lane < BLOCK // 2, before, turned))):
                    flat[q, at, pl.ds(t * BLOCK, BLOCK)] = part_q
                before = turned
            return carry

        lax.fori_loop(0, height // part, piece, 0)

    def along_cols(height, begin, end, both):
        def block(j, carry):
            at = pl.ds(pl.multiple_of(j * BLOCK, BLOCK), WINDOW)
            put = (pl.ds(0, height), pl.ds(pl.multiple_of(j * BLOCK, BLOCK), BLOCK))
            kind = jnp.where((j == 1) & (col == 0), 1, jnp.where((j == per_c) & (col == n_col - 1), 2, 0))
            x1, x2, x3 = (flat[q, pl.ds(0, height), at] for q in range(3))

            def apply(weights, to):
                got = mul(x2, weights[:, :2 * BLOCK]) + mul(x1, weights[:, :2 * BLOCK])
                small = mul(x3, weights[:, :BLOCK]) + mul(x1, weights[:, 2 * BLOCK:])
                for q, part_q in enumerate(split(got[:, :BLOCK] + (got[:, BLOCK:] + small))):
                    to[(q, *put)] = part_q

            apply(col_g[kind], mid)
            if both:
                apply(col_b[...], midb)
            return carry

        lax.fori_loop(begin, end, block, 0)

    def along_rows(weights, source, at, length):
        top = mul(weights, source[(0, *at)])
        more = mul(weights[:2 * TALL, :], source[(1, *at)])
        least = mul(weights[:TALL, :], source[(2, *at)])
        small = (top[2 * TALL:2 * TALL + length] + more[TALL:TALL + length]) + least[:length]
        return top[:length] + ((top[TALL:TALL + length] + more[:length]) + small)

    def update(start, sizes, kinds, before, shift, height, after, begin, end):
        offset = 0
        for size, kind in zip(sizes, kinds):
            def strip(n, carry, offset=offset, size=size, kind=kind):
                across = pl.ds(pl.multiple_of(n * WINDOW, WINDOW) + begin, WINDOW)
                at = (pl.ds(offset, WINDOW), across)
                chosen = jnp.where(row == (0 if kind < 4 else n_row - 1), kind, 0)
                blurred = along_rows(row_g[chosen], mid, at, size)
                if start == -64:
                    extra = along_rows(row_b[...], midb, at, size)
                    nudge[pl.ds(offset, size), across] = extra
                else:
                    extra = nudge[pl.ds(offset + start + 64, size), across]
                value = before[pl.ds(offset + shift, size), across] + STEP_GAIN * (extra - blurred)
                if start == 0:
                    after[pl.ds(offset, size), pl.ds(pl.multiple_of(n * WINDOW, WINDOW), WINDOW)] = value
                else:
                    after[pl.ds(offset, size), across] = jnp.where(
                        inside((size, WINDOW), 0, row0 + (start + offset), scene_rows)
                        & inside((size, WINDOW), 1, col0 + (n * WINDOW - EDGE), scene_cols), value, 0.0)
                return carry

            lax.fori_loop(0, (end - begin) // WINDOW, strip, 0)
            offset += size

    flatten(wide, rows, True)
    along_cols(rows, 0, cols // BLOCK, True)
    update(-64, (160, 160, 160, 160), (1, 0, 0, 4), wide, 32, rows - 64, state, 0, cols)
    flatten(state, rows - 64, False)
    along_cols(rows - 64, 0, cols // BLOCK, False)
    update(-32, (192, 192, 192), (2, 0, 5), state, 32, rows - 128, wide, 0, cols)
    flatten(wide, rows - 128, False)
    along_cols(rows - 128, 1, 1 + per_c, False)
    update(0, (192, 192, 128), (3, 0, 6), wide, 32, tile_rows, sharp, EDGE, EDGE + tile_cols)

    kept.wait()

    def collect(k, carry):
        parcel(k).wait()
        return carry

    lax.fori_loop(1, n_row, collect, 0)
    fetch = pltpu.make_async_copy(arrived.at[:, pl.ds(4 * BLOCK, TAIL), :], labels, local_sem.at[2])
    fetch.start()
    fetch.wait()
    lane = lax.broadcasted_iota(jnp.int32, (1, BLOCK), 1)
    found = jnp.zeros((1, BLOCK), jnp.int32)
    for r in range(n_row):
        for which in range(2):
            tag = labels[r][which:which + 1, :].astype(jnp.float32).astype(jnp.int32)
            found = jnp.where(tag == lane, 2 * r + which, found)
    place[...] = found


def sweeps(n_row, n_col, krow, kcol, target, observed, sentinel):
    tile_rows, tile_cols = observed.shape
    rows, cols = tile_rows + 2 * FRAME, tile_cols + 2 * EDGE
    f32, b16 = jnp.float32, jnp.bfloat16
    vmem = pl.BlockSpec(memory_space=pltpu.VMEM)
    any_ = pl.BlockSpec(memory_space=pl.ANY)
    parcel = 4 * BLOCK + TAIL
    return pl.pallas_call(
        functools.partial(sweep_kernel, n_row, n_col),
        in_specs=[any_] * 5,
        out_specs=[vmem, any_, vmem],
        out_shape=[
            jax.ShapeDtypeStruct((tile_rows, tile_cols), f32),
            jax.ShapeDtypeStruct((n_row, parcel, BLOCK), b16),
            jax.ShapeDtypeStruct((1, BLOCK), jnp.int32),
        ],
        scratch_shapes=[
            pltpu.SMEM(krow.shape, f32),
            pltpu.SMEM(kcol.shape, f32),
            pltpu.SMEM(target.shape, jnp.int32),
            pltpu.VMEM((target.size, 2 * BLOCK, BLOCK), b16),
            pltpu.VMEM((n_row, parcel, BLOCK), b16),
            pltpu.VMEM((rows, cols), f32),
            pltpu.VMEM((3, rows, cols + BLOCK), b16),
            pltpu.VMEM((3, rows + 32, cols), b16),
            pltpu.VMEM((3, rows + 32, cols), b16),
            pltpu.VMEM((rows - 64, cols), f32),
            pltpu.VMEM((rows - 64, cols), f32),
            pltpu.VMEM((WINDOW, WINDOW), f32),
            pltpu.VMEM((WINDOW, WINDOW), f32),
            pltpu.VMEM((7, 3 * TALL, WINDOW), b16),
            pltpu.VMEM((3 * TALL, WINDOW), b16),
            pltpu.VMEM((3, WINDOW, 3 * BLOCK), b16),
            pltpu.VMEM((WINDOW, 3 * BLOCK), b16),
            pltpu.VMEM((n_row, TAIL, BLOCK), b16),
            pltpu.SemaphoreType.DMA((8,)),
            pltpu.SemaphoreType.DMA((8,)),
            pltpu.SemaphoreType.DMA((n_row,)),
            pltpu.SemaphoreType.DMA((n_row,)),
            pltpu.SemaphoreType.DMA((7,)),
        ],
        compiler_params=pltpu.CompilerParams(collective_id=0, has_side_effects=True, vmem_limit_bytes=48 << 20),
        name="sweeps",
    )(krow, kcol, target, observed, sentinel)


def local(n_row, n_col, observed, kernel_rows, kernel_cols, air_temp, wind_speed, net_radiation, sentinel, block_target, land_mask):
    theta, arrived, place = sweeps(n_row, n_col, kernel_rows, kernel_cols, block_target, observed, sentinel)
    return energy(place, arrived, theta, air_temp, wind_speed, net_radiation, land_mask)


def solution(mesh):
    tile = P("row", "col")
    return jax.shard_map(
        functools.partial(local, mesh.shape["row"], mesh.shape["col"]),
        mesh=mesh,
        in_specs=(tile, P(), P(), tile, tile, tile, P(None, "row", "col"), tile, tile),
        out_specs=(tile, tile, tile),
        check_vma=False,
    )
```
